32 devices in a mesh: ctx: 32 (over z, y, x, core).
Axes of the slice: x: 2, y: 2, z: 4, core: 2. Of those that a mesh axis runs over, the one named last changes fastest.
Arguments:
- queries: bfloat16 [4096, 16, 128], P('ctx'), may hold values from -6 to 6
- keys: bfloat16 [4096, 8, 128], P('ctx'), may hold values from -5 to 5
- values: bfloat16 [4096, 8, 128], P('ctx'), may hold values from -6 to 6
- d_out: bfloat16 [4096, 16, 128], P('ctx'), may hold values from -48 to 48
Outputs:
- grad_queries: bfloat16 [4096, 16, 128], P('ctx')
- grad_keys: bfloat16 [4096, 8, 128], P('ctx')
- grad_values: bfloat16 [4096, 8, 128], P('ctx')
The draws below stay inside these ranges and needn't reach their ends.
All inputs are finite; a program needn't handle non-finite values.
Results may differ from the reference program's by a relative error of at most 0.012.
The reference program's roundings to bfloat16 on the way count: a program that leaves them out, or rounds other values in their place, can miss the bound.
Values may be sent and summed in bfloat16 or wider, within the bound.
No kernel may reach another device: no remote copies, remote signals or barrier semaphores. Data moves between devices by JAX's collectives and lax.ppermute only.
A program may use at most 64 MiB of HBM per device.

```python
import jax
import jax.numpy as jnp
from jax import lax

HEADS = 16
KV_HEADS = 8
HEAD_WIDTH = 128
WINDOW = 512
TOK_DEV = 128
TOKENS = 4096


def draw_queries(key, part):
    result = jax.random.normal(jax.random.fold_in(key, 11), (TOKENS, HEADS, HEAD_WIDTH), jnp.float32)
    result = jnp.clip(result, -5.0, 5.0)
    return result.astype(jnp.bfloat16)


def draw_keys(key, part):
    result = jax.random.normal(jax.random.fold_in(key, 13), (TOKENS, KV_HEADS, HEAD_WIDTH), jnp.float32)
    result = jnp.clip(result, -5.0, 5.0)
    return result.astype(jnp.bfloat16)


def shard_levels(stream_key, shape, shards, low, largest):
    loudness = 1.0
    for dim, parts in shards:
        heights = jax.random.uniform(jax.random.fold_in(jax.random.fold_in(stream_key, 6), dim), (parts,), jnp.float32, low / len(shards), largest / len(shards))
        loudness = loudness * jnp.repeat(jnp.exp(heights), shape[dim] // parts).reshape((-1,) + (1,) * (len(shape) - 1 - dim))
    return loudness


def gaussian(rng, dims, spread, bound, split=(), kind=jnp.bfloat16):
    drawn = spread * jax.random.normal(rng, dims, jnp.float32)
    if split:
        drawn = drawn * shard_levels(rng, dims, split, -0.22, 0.18)
    return jnp.clip(drawn, -bound, bound).astype(kind)


def setup_inputs(seed: int = 0) -> dict:
    key_of = jax.random.split(jax.random.key(seed), 5)
    queries = draw_queries(jax.random.fold_in(key_of[4], 71), 0)
    keys = draw_keys(jax.random.fold_in(key_of[4], 71), 0)
    values = gaussian(key_of[2], (TOKENS, KV_HEADS, HEAD_WIDTH), 1.0, 6.0, ((0, 32),))
    d_out = gaussian(key_of[3], (TOKENS, HEADS, HEAD_WIDTH), 8.0, 48.0, ((0, 32),))
    return dict(queries=queries, keys=keys, values=values, d_out=d_out)


score_scale = 168.0 ** -0.5


def block_grads(queries_blk, keys_win, values_win, block_gradient, row_start):
    row_count = queries_blk.shape[0]
    key_span = keys_win.shape[0]
    group_size = HEADS // KV_HEADS
    grouped = queries_blk.reshape(row_count, KV_HEADS, group_size, HEAD_WIDTH).astype(jnp.float32)
    gradient_per_group = block_gradient.reshape(row_count, KV_HEADS, group_size, HEAD_WIDTH).astype(jnp.float32)
    keys_wide = keys_win.astype(jnp.float32)
    widened_values = values_win.astype(jnp.float32)
    scores = jnp.einsum("tgre,jge->grtj", grouped, keys_wide) * score_scale
    query_pos = row_start + jnp.arange(row_count, dtype=jnp.int32)
    key_pos = row_start - WINDOW + jnp.arange(key_span, dtype=jnp.int32)
    distance = query_pos[:, None] - key_pos[None, :]
    visible = (distance >= 0) & (distance < WINDOW) & (key_pos[None, :] >= 0)
    scores = jnp.where(visible, scores, -jnp.inf)
    row_max = jnp.max(scores, axis=-1, keepdims=True)
    row_sum = jnp.sum(jnp.exp(scores - row_max), axis=-1, keepdims=True)
    log_total = row_max + jnp.log(row_sum)
    probability = jnp.exp(scores - log_total)
    probs_low = lax.optimization_barrier(probability.astype(jnp.bfloat16))
    attention_result_rows = jnp.einsum("grtj,jge->tgre", probs_low.astype(jnp.float32), widened_values).astype(jnp.bfloat16)
    attention_result_rows = lax.optimization_barrier(attention_result_rows)
    row_dot_product = jnp.einsum("vwhn,vwhn->whv", gradient_per_group, attention_result_rows.astype(jnp.float32))
    grad_probs = jnp.einsum("tgre,jge->grtj", gradient_per_group, widened_values)
    grad_scores = lax.optimization_barrier((probability * (grad_probs - row_dot_product[..., None])).astype(jnp.bfloat16))
    grad_scores_wide = grad_scores.astype(jnp.float32)
    query_gradient = (jnp.einsum("grtj,jge->tgre", grad_scores_wide, keys_wide) * score_scale).astype(jnp.bfloat16)
    grad_key = jnp.einsum("grtj,tgre->jge", grad_scores_wide, grouped) * score_scale
    grad_value = jnp.einsum("grtj,tgre->jge", probs_low.astype(jnp.float32), gradient_per_group)
    return query_gradient.reshape(row_count, HEADS, HEAD_WIDTH), grad_key, grad_value


def reference(queries, keys, values, d_out):
    blocks = TOKENS // TOK_DEV
    key_span = WINDOW + TOK_DEV
    front_pad = jnp.zeros((WINDOW, KV_HEADS, HEAD_WIDTH), keys.dtype)
    padded_keys = jnp.concatenate([front_pad, keys], axis=0)
    values_pad = jnp.concatenate([front_pad, values], axis=0)

    def advance(running, block_index):
        row_start = (block_index * TOK_DEV).astype(jnp.int32)
        queries_blk = lax.dynamic_slice_in_dim(queries, row_start, TOK_DEV, 0)
        block_gradient = lax.dynamic_slice_in_dim(d_out, row_start, TOK_DEV, 0)
        keys_win = lax.dynamic_slice_in_dim(padded_keys, row_start, key_span, 0)
        values_win = lax.dynamic_slice_in_dim(values_pad, row_start, key_span, 0)
        query_gradient, grad_key, grad_value = block_grads(queries_blk, keys_win, values_win, block_gradient, row_start)
        key_acc, value_acc = running
        key_acc = lax.dynamic_update_slice_in_dim(key_acc, lax.dynamic_slice_in_dim(key_acc, row_start, key_span, 0) + grad_key, row_start, 0)
        value_acc = lax.dynamic_update_slice_in_dim(value_acc, lax.dynamic_slice_in_dim(value_acc, row_start, key_span, 0) + grad_value, row_start, 0)
        return (key_acc, value_acc), query_gradient

    empty_totals = jnp.zeros((TOKENS + WINDOW, KV_HEADS, HEAD_WIDTH), jnp.float32)
    (key_acc, value_acc), grad_blocks = lax.scan(advance, (empty_totals, empty_totals), jnp.arange(blocks, dtype=jnp.int32))
    grad_queries = grad_blocks.reshape(TOKENS, HEADS, HEAD_WIDTH)
    return grad_queries, key_acc[WINDOW:].astype(jnp.bfloat16), value_acc[WINDOW:].astype(jnp.bfloat16)
```

```python
import functools
import math

import jax
import jax.numpy as jnp
from jax import lax
from jax.experimental import pallas as pl
from jax.experimental.pallas import tpu as pltpu
from jax.sharding import PartitionSpec as P

WINDOW = 512
SCORE_SCALE = 168.0 ** -0.5
LOG2E = math.log2(math.e)
NEG = -1e30
VMEM_LIMIT = 48 * 1024 * 1024

NT = (((1,), (1,)), ((), ()))
NN = (((1,), (0,)), ((), ()))
TN = (((0,), (0,)), ((), ()))


def dot(a, b, dims):
    return lax.dot_general(a, b, dims, preferred_element_type=jnp.float32)


def swap(a, by):
    n = lax.axis_size("ctx")
    return lax.ppermute(a, "ctx", [(i, i ^ by) for i in range(n)])


def shift(a, by):
    n = lax.axis_size("ctx")
    return lax.ppermute(a, "ctx", [(i, i + by) for i in range(n) if 0 <= i + by < n])


def split_heads_kernel(place, a_ref, b_ref, keep_ref, send_ref, wide):
    tok, heads, width = a_ref.shape
    half = heads // 2
    x = place[0]
    for s, ref in enumerate((a_ref, b_ref)):
        wide[s] = ref[...].astype(jnp.float32).reshape(tok * heads, width)
        for j in range(half):
            low = wide[s, pl.ds(j, tok, stride=heads), :]
            high = wide[s, pl.ds(half + j, tok, stride=heads), :]
            keep_ref[s, j] = jnp.where(x == 0, low, high).astype(jnp.bfloat16)
            send_ref[s, j] = jnp.where(x == 0, high, low).astype(jnp.bfloat16)


def split_heads(place, a, b):
    tok, heads, width = a.shape
    out = jax.ShapeDtypeStruct((2, heads // 2, tok, width), jnp.bfloat16)
    return pl.pallas_call(
        split_heads_kernel,
        out_shape=(out, out),
        in_specs=[pl.BlockSpec(memory_space=pltpu.SMEM)] + [pl.BlockSpec(memory_space=pltpu.VMEM)] * 2,
        out_specs=(pl.BlockSpec(memory_space=pltpu.VMEM),) * 2,
        scratch_shapes=[pltpu.VMEM((2, tok * heads, width), jnp.float32)],
        compiler_params=pltpu.CompilerParams(vmem_limit_bytes=VMEM_LIMIT),
        name="split_heads",
    )(place, a, b)


def grads_kernel(
    place, keep_q, sent_q, ko, xo, mko, mxo, k1, k2, mk1, mk2,
    dq_keep, dq_send, prev_here, prev_mate, own_here, own_mate,
    kv, dkv,
):
    _, _, tok, width = ko.shape
    x, c, first = place[0], place[1], place[2]
    heads = keep_q.shape[1]
    mine, other = 2 * x + c, 2 * (1 - x) + c
    mate_mine, mate_other = 2 * x + 1 - c, 2 * (1 - x) + 1 - c
    blocks = WINDOW // tok

    def rows(slot):
        return pl.ds(pl.multiple_of(slot * tok, tok), tok)

    for ref, slot in (
        (k1, mine), (k2, other), (mk1, mate_mine), (mk2, mate_other),
        (ko, blocks + mine), (xo, blocks + other), (mko, blocks + mate_mine), (mxo, blocks + mate_other),
    ):
        for s in range(2):
            kv[s, rows(slot), :] = ref[s, 0]
    dkv[...] = jnp.zeros_like(dkv)

    query = lax.broadcasted_iota(jnp.int32, (heads * tok, tok), 0) % tok
    key = lax.broadcasted_iota(jnp.int32, (heads * tok, tok), 1)
    before, upto = key > query, key <= query

    for q_ref, block, dq_ref in ((keep_q, mine, dq_keep), (sent_q, other, dq_send)):
        window = pl.ds(pl.multiple_of(block * tok, tok), WINDOW + tok)
        q = q_ref[0].reshape(heads * tok, width)
        do = q_ref[1].reshape(heads * tok, width)
        k = kv[0, window, :]
        v = kv[1, window, :]
        scores = dot(q, k, NT) * (SCORE_SCALE * LOG2E)
        parts = []
        for t in range(blocks + 1):
            part = scores[:, t * tok : (t + 1) * tok]
            if t < blocks:
                hidden = jnp.logical_and(first == 1, block + t < blocks)
                part = part + jnp.where(hidden, NEG, 0.0)
            if t == 0:
                part = jnp.where(before, part, NEG)
            if t == blocks:
                part = jnp.where(upto, part, NEG)
            parts.append(part)
        top = jnp.max(functools.reduce(jnp.maximum, parts), axis=1, keepdims=True)
        parts = [jnp.exp2(part - top) for part in parts]
        total = jnp.sum(sum(parts[1:], parts[0]), axis=1, keepdims=True)
        inverse = 1.0 / total
        prob = jnp.concatenate([part * inverse for part in parts], axis=1)
        low = prob.astype(jnp.bfloat16)
        attended = dot(low, v, NN).astype(jnp.bfloat16)
        row_dot = jnp.sum(do.astype(jnp.float32) * attended.astype(jnp.float32), axis=1, keepdims=True)
        ds = (prob * (dot(do, v, NT) - row_dot)).astype(jnp.bfloat16)
        dq = dot(ds, k, NN) * SCORE_SCALE
        dq_ref[...] = dq.astype(jnp.bfloat16).reshape(heads, tok, width)
        dkv[0, window, :] += dot(ds, q, TN)
        dkv[1, window, :] += dot(low, do, TN)

    for s, scale in enumerate((SCORE_SCALE, 1.0)):
        for ref, base, pair in (
            (prev_here, 0, (mine, other)),
            (prev_mate, 0, (mate_mine, mate_other)),
            (own_here, blocks, (mine, other)),
            (own_mate, blocks, (mate_mine, mate_other)),
        ):
            for k_, slot in enumerate(pair):
                ref[k_, s, 0] = (dkv[s, rows(base + slot), :] * scale).astype(ref.dtype)


def grads(place, keep_q, sent_q, *kvs):
    _, groups, tok, width = kvs[0].shape
    q_heads = keep_q.shape[1]
    per = q_heads // groups
    bf, f32 = jnp.bfloat16, jnp.float32
    q_spec = pl.BlockSpec((2, per, tok, width), lambda g: (0, g, 0, 0))
    kv_spec = pl.BlockSpec((2, 1, tok, width), lambda g: (0, g, 0, 0))
    dq_spec = pl.BlockSpec((per, tok, width), lambda g: (g, 0, 0))
    dkv_spec = pl.BlockSpec((2, 2, 1, tok, width), lambda g: (0, 0, g, 0, 0))
    dq_shape = jax.ShapeDtypeStruct((q_heads, tok, width), bf)
    dkv_shape = functools.partial(jax.ShapeDtypeStruct, (2, 2, groups, tok, width))
    return pl.pallas_call(
        grads_kernel,
        grid=(groups,),
        out_shape=(dq_shape, dq_shape, dkv_shape(f32), dkv_shape(bf), dkv_shape(f32), dkv_shape(bf)),
        in_specs=[pl.BlockSpec(memory_space=pltpu.SMEM)] + [q_spec] * 2 + [kv_spec] * 8,
        out_specs=(dq_spec, dq_spec) + (dkv_spec,) * 4,
        scratch_shapes=[
            pltpu.VMEM((2, 2 * WINDOW, width), bf),
            pltpu.VMEM((2, 2 * WINDOW, width), f32),
        ],
        compiler_params=pltpu.CompilerParams(vmem_limit_bytes=VMEM_LIMIT),
        name="window_grads",
    )(place, keep_q, sent_q, *kvs)


def join_heads_kernel(place, keep_ref, sent_ref, out_ref, wide):
    tok, heads, width = out_ref.shape
    half = heads // 2
    x = place[0]
    for j in range(half):
        keep = keep_ref[j].astype(jnp.float32)
        sent = sent_ref[j].astype(jnp.float32)
        wide[pl.ds(j, tok, stride=heads), :] = jnp.where(x == 0, keep, sent)
        wide[pl.ds(half + j, tok, stride=heads), :] = jnp.where(x == 0, sent, keep)
    out_ref[...] = wide[...].reshape(tok, heads, width).astype(out_ref.dtype)


def join_heads(place, keep, sent):
    half, tok, width = keep.shape
    return pl.pallas_call(
        join_heads_kernel,
        out_shape=jax.ShapeDtypeStruct((tok, 2 * half, width), jnp.bfloat16),
        in_specs=[pl.BlockSpec(memory_space=pltpu.SMEM)] + [pl.BlockSpec(memory_space=pltpu.VMEM)] * 2,
        out_specs=pl.BlockSpec(memory_space=pltpu.VMEM),
        scratch_shapes=[pltpu.VMEM((tok * 2 * half, width), jnp.float32)],
        compiler_params=pltpu.CompilerParams(vmem_limit_bytes=VMEM_LIMIT),
        name="join_heads",
    )(place, keep, sent)


def body(queries, keys, values, d_out):
    tok = queries.shape[0]
    quad = WINDOW // tok
    assert quad == 4 and lax.axis_size("ctx") % quad == 0
    me = lax.axis_index("ctx")
    x, c, first = (me // 2) % 2, me % 2, (me < quad).astype(jnp.int32)
    place = jnp.stack([x, c, first]).astype(jnp.int32)
    bf, f32 = jnp.bfloat16, jnp.float32

    kv_keep, kv_send = split_heads(place, keys, values)
    kv_x = swap(kv_send, 2)
    kv_1 = shift(kv_keep, quad)
    q_keep, q_send = split_heads(place, queries, d_out)
    q_x = swap(q_send, 2)
    kv_2 = shift(kv_x, quad)
    mates = [swap(a, 1) for a in (kv_keep, kv_x, kv_1, kv_2)]

    dq_keep, dq_send, prev_here, prev_mate, own_here, own_mate = grads(
        place, q_keep, q_x, kv_keep, kv_x, mates[0], mates[1], kv_1, kv_2, mates[2], mates[3]
    )
    prev_sum = (prev_here + swap(prev_mate, 1).astype(f32)).astype(bf)
    back_2 = shift(prev_sum[1], -quad)
    back_1 = shift(prev_sum[0], -quad)
    own_sum = own_here + swap(own_mate, 1).astype(f32)
    other = (own_sum[1] + back_2.astype(f32)).astype(bf)
    dkv_x = swap(other, 2)
    dq_x = swap(dq_send, 2)
    mine = (own_sum[0] + back_1.astype(f32)).astype(bf)
    return (
        join_heads(place, dq_keep, dq_x),
        join_heads(place, mine[0], dkv_x[0]),
        join_heads(place, mine[1], dkv_x[1]),
    )


def solution(mesh):
    spec = P("ctx", None, None)
    return jax.shard_map(
        body,
        mesh=mesh,
        in_specs=(spec,) * 4,
        out_specs=(spec,) * 3,
        check_vma=False,
    )
```

```python
import functools
import math

import jax
import jax.numpy as jnp
from jax import lax
from jax.experimental import pallas as pl
from jax.experimental.pallas import tpu as pltpu
from jax.sharding import PartitionSpec as P

WINDOW = 512
SCORE_SCALE = 168.0 ** -0.5
LOG2E = math.log2(math.e)
NEG = -1e30
VMEM_LIMIT = 48 * 1024 * 1024

NT = (((1,), (1,)), ((), ()))
NN = (((1,), (0,)), ((), ()))


def dot(a, b, dims):
    return lax.dot_general(a, b, dims, preferred_element_type=jnp.float32)


def swap(a, by):
    n = lax.axis_size("ctx")
    return lax.ppermute(a, "ctx", [(i, i ^ by) for i in range(n)])


def shift(a, by, wrap=False):
    n = lax.axis_size("ctx")
    pairs = [(i, (i + by) % n) for i in range(n) if wrap or 0 <= i + by < n]
    return lax.ppermute(a, "ctx", pairs)


def after(a, *others):
    return lax.optimization_barrier((a, *others))[0]


def split_heads_kernel(place, *refs):
    wide = refs[-1]
    ins = [refs[0].at[0], refs[0].at[1]] if len(refs[0].shape) == 4 else refs[:2]
    keep_ref, *sends = refs[1:-1] if len(refs[0].shape) == 4 else refs[2:-1]
    tok, heads, width = ins[0].shape
    half = heads // 2
    part = half // len(sends)
    x = place[0]
    for s, ref in enumerate(ins):
        wide[s] = ref[...].astype(jnp.float32).reshape(tok * heads, width)
        for j in range(half):
            low = wide[s, pl.ds(j, tok, stride=heads), :]
            high = wide[s, pl.ds(half + j, tok, stride=heads), :]
            keep_ref[s, j] = jnp.where(x == 0, low, high).astype(jnp.bfloat16)
            sends[j // part][s, j % part] = jnp.where(x == 0, high, low).astype(jnp.bfloat16)


def split_heads(place, chunks, *arrays):
    tok, heads, width = arrays[0].shape[-3:]
    shapes = [jax.ShapeDtypeStruct((2, heads // 2 // k, tok, width), jnp.bfloat16) for k in [1] + [chunks] * chunks]
    vmem = pl.BlockSpec(memory_space=pltpu.VMEM)
    return pl.pallas_call(
        split_heads_kernel,
        out_shape=tuple(shapes),
        in_specs=[pl.BlockSpec(memory_space=pltpu.SMEM)] + [vmem] * len(arrays),
        out_specs=(vmem,) * len(shapes),
        scratch_shapes=[pltpu.VMEM((2, tok * heads, width), jnp.float32)],
        compiler_params=pltpu.CompilerParams(vmem_limit_bytes=VMEM_LIMIT),
        name="split_heads",
    )(place, *arrays)


def grads_kernel(
    start, groups, place, keep_q, sent_q, ko, xo, mko, mxo, k1, k2, mk1, mk2,
    dq_keep, dq_send, prev_here, prev_mate, own_here, own_mate,
    kv,
):
    _, all_groups, tok, width = ko.shape
    heads = keep_q.shape[1] // all_groups
    x, c, first = place[0], place[1], place[2]
    blocks = WINDOW // tok
    span = WINDOW + tok
    reach = (2 * blocks - 1) * tok
    mine, other = 2 * x + c, 2 * (1 - x) + c
    mate_mine, mate_other = 2 * x + 1 - c, 2 * (1 - x) + 1 - c
    for ref, slot in (
        (k1, mine), (k2, other), (mk1, mate_mine), (mk2, mate_other),
        (ko, blocks + mine), (xo, blocks + other), (mko, blocks + mate_mine), (mxo, blocks + mate_other),
    ):
        kv[:, :, pl.ds(pl.multiple_of(slot * tok, tok), tok), :] = ref[:, start : start + groups]
    rows = pl.ds(pl.multiple_of(c * tok, tok), reach)
    key = lax.broadcasted_iota(jnp.int32, (tok, heads * tok), 0)
    query = lax.broadcasted_iota(jnp.int32, (tok, heads * tok), 1) % tok
    before, upto = key > query, key <= query

    def load(g):
        k, v = kv[0, g, rows, :], kv[1, g, rows, :]
        qs = []
        for xx in range(2):
            pair = []
            for s in range(2):
                mine_of = pl.ds((start + g) * heads, heads)
                keep, sent = keep_q[s, mine_of], sent_q[s, mine_of]
                pair.append(jnp.where(x == xx, keep, sent).reshape(heads * tok, width))
            qs.append(pair)
        return k, v, k.T, qs

    def products(state, xx):
        k, v, kt, qs = state
        q, do = qs[xx]
        win = slice(xx * 2 * tok, xx * 2 * tok + span)
        return dot(k[win], q, NT), dot(v[win], do, NT)

    def weights(state, xx, scores, gp):
        parts = []
        for t in range(blocks + 1):
            part = scores[t * tok : (t + 1) * tok] * (SCORE_SCALE * LOG2E)
            if t < blocks:
                hidden = jnp.logical_and(first == 1, 2 * xx + c + t < blocks)
                part = part + jnp.where(hidden, NEG, 0.0)
            if t == 0:
                part = jnp.where(before, part, NEG)
            if t == blocks:
                part = jnp.where(upto, part, NEG)
            parts.append(part)
        top = jnp.max(functools.reduce(jnp.maximum, parts), axis=0, keepdims=True)
        parts = [jnp.exp2(part - top) for part in parts]
        gps = [gp[t * tok : (t + 1) * tok] for t in range(blocks + 1)]
        total = jnp.sum(sum(parts[1:], parts[0]), axis=0, keepdims=True)
        mixed = [p * g for p, g in zip(parts, gps)]
        inverse = 1.0 / total
        row_dot = jnp.sum(sum(mixed[1:], mixed[0]), axis=0, keepdims=True) * inverse
        parts = [part * inverse for part in parts]
        low = jnp.concatenate([p.astype(jnp.bfloat16) for p in parts], axis=0)
        ds = jnp.concatenate([(p * (g - row_dot)).astype(jnp.bfloat16) for p, g in zip(parts, gps)], axis=0)
        return low, ds

    def outputs(g, state, sides):
        k, v, kt, qs = state
        dqs = []
        for xx in range(2):
            win = slice(xx * 2 * tok, xx * 2 * tok + span)
            dqs.append((dot(kt[:, win], sides[xx][1], NN) * SCORE_SCALE).T.astype(jnp.bfloat16).reshape(heads, tok, width))
        hs = pl.ds(g * heads, heads)
        dq_keep[hs] = jnp.where(x == 0, dqs[0], dqs[1])
        dq_send[hs] = jnp.where(x == 0, dqs[1], dqs[0])
        cut = span - 2 * tok
        for s, scale in enumerate((SCORE_SCALE, 1.0)):
            w0, w1 = sides[0][1 - s], sides[1][1 - s]
            r0, r1 = qs[0][s], qs[1][s]
            early = dot(w0[: 2 * tok], r0, NN)
            both = dot(w0[2 * tok :], r0, NN) + dot(w1[:cut], r1, NN)
            late = dot(w1[cut:], r1, NN)
            got = jnp.concatenate([early, both, late], axis=0) * scale
            for t in range(0, 2 * blocks - 1, 2):
                ref, xx = (prev_here, t // 2) if t < blocks else (own_here, (t - blocks) // 2)
                ref[xx ^ x, s, g] = got[t * tok : (t + 1) * tok].astype(ref.dtype)
            odd = [got[t * tok : (t + 1) * tok].astype(jnp.bfloat16) for t in (1, 3, 5)]
            zero = jnp.zeros_like(odd[0])
            low_core = c == 0
            four = [
                jnp.where(low_core, odd[0], zero),
                jnp.where(low_core, odd[1], odd[0]),
                jnp.where(low_core, odd[2], odd[1]),
                jnp.where(low_core, zero, odd[2]),
            ]
            for xx in range(2):
                prev_mate[xx ^ x, s, g] = four[xx]
                own_mate[xx ^ x, s, g] = four[2 + xx]

    flow = [(g, xx) for g in range(groups) for xx in range(2)]
    states = {0: load(0)}
    ready = products(states[0], 0)
    sides = {}
    for i, (g, xx) in enumerate(flow):
        now = ready
        if i + 1 < len(flow):
            ng, nx = flow[i + 1]
            if ng not in states:
                states[ng] = load(ng)
            ready = products(states[ng], nx)
        if xx == 0 and g > 0:
            outputs(g - 1, states.pop(g - 1), sides.pop(g - 1))
        sides.setdefault(g, []).append(weights(states[g], xx, *now))
    outputs(groups - 1, states[groups - 1], sides[groups - 1])

def grads(start, groups, place, keep_q, sent_q, *kvs):
    _, all_groups, tok, width = kvs[0].shape
    heads = keep_q.shape[1] // all_groups
    bf, f32 = jnp.bfloat16, jnp.float32
    dq_shape = jax.ShapeDtypeStruct((groups * heads, tok, width), bf)
    dkv_shape = functools.partial(jax.ShapeDtypeStruct, (2, 2, groups, tok, width))
    vmem = pl.BlockSpec(memory_space=pltpu.VMEM)
    return pl.pallas_call(
        functools.partial(grads_kernel, start, groups),
        out_shape=(dq_shape, dq_shape, dkv_shape(f32), dkv_shape(bf), dkv_shape(f32), dkv_shape(bf)),
        in_specs=[pl.BlockSpec(memory_space=pltpu.SMEM)] + [vmem] * 10,
        out_specs=(vmem,) * 6,
        scratch_shapes=[pltpu.VMEM((2, groups, 2 * WINDOW, width), bf)],
        compiler_params=pltpu.CompilerParams(vmem_limit_bytes=VMEM_LIMIT),
        cost_estimate=pl.CostEstimate(flops=1, bytes_accessed=1, transcendentals=0),
        name="window_grads",
    )(place, keep_q, sent_q, *kvs)


def join_heads_kernel(count, place, *refs):
    outs, wide = refs[-1 - count : -1], refs[-1]
    ins = refs[: -1 - count]
    tok, heads, width = outs[0].shape
    half = heads // 2
    chunks = len(ins) // 2
    part = half // chunks
    x = place[0]
    for s, out in enumerate(outs):
        for j in range(half):
            keep = ins[j // part][s, j % part].astype(jnp.float32)
            sent = ins[chunks + j // part][s, j % part].astype(jnp.float32)
            wide[s, pl.ds(j, tok, stride=heads), :] = jnp.where(x == 0, keep, sent)
            wide[s, pl.ds(half + j, tok, stride=heads), :] = jnp.where(x == 0, sent, keep)
        out[...] = wide[s].reshape(tok, heads, width).astype(out.dtype)


def join_heads(place, keeps, sents):
    count, part, tok, width = keeps[0].shape
    heads = 2 * part * len(keeps)
    vmem = pl.BlockSpec(memory_space=pltpu.VMEM)
    return pl.pallas_call(
        functools.partial(join_heads_kernel, count),
        out_shape=(jax.ShapeDtypeStruct((tok, heads, width), jnp.bfloat16),) * count,
        in_specs=[pl.BlockSpec(memory_space=pltpu.SMEM)] + [vmem] * (2 * len(keeps)),
        out_specs=(vmem,) * count,
        scratch_shapes=[pltpu.VMEM((count, tok * heads, width), jnp.float32)],
        compiler_params=pltpu.CompilerParams(vmem_limit_bytes=VMEM_LIMIT),
        name="join_heads",
    )(place, *keeps, *sents)


def body(queries, keys, values, d_out):
    tok = queries.shape[0]
    quad = WINDOW // tok
    assert quad == 4 and lax.axis_size("ctx") % quad == 0
    me = lax.axis_index("ctx")
    x, c, first = (me // 2) % 2, me % 2, (me < quad).astype(jnp.int32)
    place = jnp.stack([x, c, first]).astype(jnp.int32)
    bf, f32 = jnp.bfloat16, jnp.float32
    chunks = 2

    kv_keep, kv_send = split_heads(place, 1, jnp.stack([keys, values]))
    q_keep, q_send = split_heads(place, 1, queries, d_out)
    kv_x = swap(kv_send, 2)
    kv_1 = shift(kv_keep, quad, wrap=True)
    q_x = swap(q_send, 2)
    kv_2 = shift(kv_x, quad)
    mates = [swap(after(a, kv_1), 1) for a in (kv_keep, kv_x)]
    mates += [swap(kv_1, 1), swap(kv_2, 1)]
    per = kv_keep.shape[1] // chunks

    dq_keep, dq_x, mine, dkv_x = [], [], [], []
    for i in range(chunks):
        keep, send, prev_here, prev_mate, own_here, own_mate = grads(
            i * per, per, place, q_keep, q_x,
            kv_keep, kv_x, mates[0], mates[1], kv_1, kv_2, mates[2], mates[3],
        )
        if i:
            own_mate = after(own_mate, back)
        prev_sum = (prev_here + swap(prev_mate, 1).astype(f32)).astype(bf)
        back = shift(prev_sum, -quad, wrap=i + 1 < chunks)
        own_sum = own_here + swap(own_mate, 1).astype(f32) + back.astype(f32)
        dkv_x.append(swap(own_sum[1].astype(bf), 2))
        mine.append(own_sum[0].astype(bf))
        dq_keep.append(keep[None])
        dq_x.append(swap(after(send, prev_sum), 2)[None])
    (dq,) = join_heads(place, dq_keep, dq_x)
    dk, dv = join_heads(place, mine, dkv_x)
    return dq, dk, dv


def solution(mesh):
    spec = P("ctx", None, None)
    return jax.shard_map(
        body,
        mesh=mesh,
        in_specs=(spec,) * 4,
        out_specs=(spec,) * 3,
        check_vma=False,
    )
```

```python
import functools
import math

import jax
import jax.numpy as jnp
from jax import lax
from jax.experimental import pallas as pl
from jax.experimental.pallas import tpu as pltpu
from jax.sharding import PartitionSpec as P

WINDOW = 512
SCORE_SCALE = 168.0 ** -0.5
LOG2E = math.log2(math.e)
NEG = -1e30
VMEM_LIMIT = 48 * 1024 * 1024

NT = (((1,), (1,)), ((), ()))
NN = (((1,), (0,)), ((), ()))


def dot(a, b, dims):
    return lax.dot_general(a, b, dims, preferred_element_type=jnp.float32)


def swap(a, by):
    n = lax.axis_size("ctx")
    return lax.ppermute(a, "ctx", [(i, i ^ by) for i in range(n)])


def shift(a, by, wrap=False):
    n = lax.axis_size("ctx")
    pairs = [(i, (i + by) % n) for i in range(n) if wrap or 0 <= i + by < n]
    return lax.ppermute(a, "ctx", pairs)


def after(a, *others):
    return lax.optimization_barrier((a, *others))[0]


def split_heads(x, a, b):
    both = jnp.stack([a, b]).transpose(0, 2, 1, 3)
    half = a.shape[1] // 2
    return [lax.dynamic_slice_in_dim(both, half * side, half, 1) for side in (x, 1 - x)]


def grads_kernel(
    start, groups, place, keep_q, sent_q, ko, xo, mko, mxo, k1, k2, mk1, mk2,
    dq_keep, dq_send, prev_here, prev_mate, own_here, own_mate,
    kv,
):
    _, all_groups, tok, width = ko.shape
    heads = keep_q.shape[1] // all_groups
    x, c, first = place[0], place[1], place[2]
    blocks = WINDOW // tok
    span = WINDOW + tok
    reach = (2 * blocks - 1) * tok
    mine, other = 2 * x + c, 2 * (1 - x) + c
    mate_mine, mate_other = 2 * x + 1 - c, 2 * (1 - x) + 1 - c
    for ref, slot in (
        (k1, mine), (k2, other), (mk1, mate_mine), (mk2, mate_other),
        (ko, blocks + mine), (xo, blocks + other), (mko, blocks + mate_mine), (mxo, blocks + mate_other),
    ):
        kv[:, :, pl.ds(pl.multiple_of(slot * tok, tok), tok), :] = ref[:, start : start + groups]
    rows = pl.ds(pl.multiple_of(c * tok, tok), reach)
    key = lax.broadcasted_iota(jnp.int32, (tok, heads * tok), 0)
    query = lax.broadcasted_iota(jnp.int32, (tok, heads * tok), 1) % tok
    before, upto = key > query, key <= query

    def load(g):
        k, v = kv[0, g, rows, :], kv[1, g, rows, :]
        qs = []
        for xx in range(2):
            pair = []
            for s in range(2):
                mine_of = pl.ds((start + g) * heads, heads)
                keep, sent = keep_q[s, mine_of], sent_q[s, mine_of]
                pair.append(jnp.where(x == xx, keep, sent).reshape(heads * tok, width))
            qs.append(pair)
        return k, v, k.T, qs

    def products(state, xx):
        k, v, kt, qs = state
        q, do = qs[xx]
        win = slice(xx * 2 * tok, xx * 2 * tok + span)
        return dot(k[win], q, NT), dot(v[win], do, NT)

    def weights(state, xx, scores, gp):
        parts = []
        for t in range(blocks + 1):
            part = scores[t * tok : (t + 1) * tok] * (SCORE_SCALE * LOG2E)
            if t < blocks:
                hidden = jnp.logical_and(first == 1, 2 * xx + c + t < blocks)
                part = part + jnp.where(hidden, NEG, 0.0)
            if t == 0:
                part = jnp.where(before, part, NEG)
            if t == blocks:
                part = jnp.where(upto, part, NEG)
            parts.append(part)
        top = jnp.max(functools.reduce(jnp.maximum, parts), axis=0, keepdims=True)
        parts = [jnp.exp2(part - top) for part in parts]
        gps = [gp[t * tok : (t + 1) * tok] for t in range(blocks + 1)]
        total = jnp.sum(sum(parts[1:], parts[0]), axis=0, keepdims=True)
        mixed = [p * g for p, g in zip(parts, gps)]
        inverse = 1.0 / total
        row_dot = jnp.sum(sum(mixed[1:], mixed[0]), axis=0, keepdims=True) * inverse
        parts = [part * inverse for part in parts]
        low = jnp.concatenate([p.astype(jnp.bfloat16) for p in parts], axis=0)
        ds = jnp.concatenate([(p * (g - row_dot)).astype(jnp.bfloat16) for p, g in zip(parts, gps)], axis=0)
        return low, ds

    def outputs(g, state, sides):
        k, v, kt, qs = state
        dqs = []
        for xx in range(2):
            win = slice(xx * 2 * tok, xx * 2 * tok + span)
            dqs.append((dot(kt[:, win], sides[xx][1], NN) * SCORE_SCALE).T.astype(jnp.bfloat16).reshape(heads, tok, width))
        hs = pl.ds(g * heads, heads)
        dq_keep[hs] = jnp.where(x == 0, dqs[0], dqs[1])
        dq_send[hs] = jnp.where(x == 0, dqs[1], dqs[0])
        cut = span - 2 * tok
        for s, scale in enumerate((SCORE_SCALE, 1.0)):
            w0, w1 = sides[0][1 - s], sides[1][1 - s]
            r0, r1 = qs[0][s], qs[1][s]
            early = dot(w0[: 2 * tok], r0, NN)
            both = dot(w0[2 * tok :], r0, NN) + dot(w1[:cut], r1, NN)
            late = dot(w1[cut:], r1, NN)
            got = jnp.concatenate([early, both, late], axis=0) * scale
            for t in range(0, 2 * blocks - 1, 2):
                ref, xx = (prev_here, t // 2) if t < blocks else (own_here, (t - blocks) // 2)
                ref[xx ^ x, s, g] = got[t * tok : (t + 1) * tok].astype(ref.dtype)
            odd = [got[t * tok : (t + 1) * tok].astype(jnp.bfloat16) for t in (1, 3, 5)]
            zero = jnp.zeros_like(odd[0])
            low_core = c == 0
            four = [
                jnp.where(low_core, odd[0], zero),
                jnp.where(low_core, odd[1], odd[0]),
                jnp.where(low_core, odd[2], odd[1]),
                jnp.where(low_core, zero, odd[2]),
            ]
            for xx in range(2):
                prev_mate[xx ^ x, s, g] = four[xx]
                own_mate[xx ^ x, s, g] = four[2 + xx]

    flow = [(g, xx) for g in range(groups) for xx in range(2)]
    states = {0: load(0)}
    ready = products(states[0], 0)
    sides = {}
    for i, (g, xx) in enumerate(flow):
        now = ready
        if i + 1 < len(flow):
            ng, nx = flow[i + 1]
            if ng not in states:
                states[ng] = load(ng)
            ready = products(states[ng], nx)
        if xx == 0 and g > 0:
            outputs(g - 1, states.pop(g - 1), sides.pop(g - 1))
        sides.setdefault(g, []).append(weights(states[g], xx, *now))
    outputs(groups - 1, states[groups - 1], sides[groups - 1])

def grads(start, groups, place, keep_q, sent_q, *kvs):
    _, all_groups, tok, width = kvs[0].shape
    heads = keep_q.shape[1] // all_groups
    bf, f32 = jnp.bfloat16, jnp.float32
    dq_shape = jax.ShapeDtypeStruct((groups * heads, tok, width), bf)
    dkv_shape = functools.partial(jax.ShapeDtypeStruct, (2, 2, groups, tok, width))
    vmem = pl.BlockSpec(memory_space=pltpu.VMEM)
    return pl.pallas_call(
        functools.partial(grads_kernel, start, groups),
        out_shape=(dq_shape, dq_shape, dkv_shape(f32), dkv_shape(bf), dkv_shape(f32), dkv_shape(bf)),
        in_specs=[pl.BlockSpec(memory_space=pltpu.SMEM)] + [vmem] * 10,
        out_specs=(vmem,) * 6,
        scratch_shapes=[pltpu.VMEM((2, groups, 2 * WINDOW, width), bf)],
        compiler_params=pltpu.CompilerParams(vmem_limit_bytes=VMEM_LIMIT),
        cost_estimate=pl.CostEstimate(flops=1, bytes_accessed=1, transcendentals=0),
        name="window_grads",
    )(place, keep_q, sent_q, *kvs)


def join_heads_kernel(count, place, *refs):
    outs, wide = refs[-1 - count : -1], refs[-1]
    ins = refs[: -1 - count]
    tok, heads, width = outs[0].shape
    half = heads // 2
    chunks = len(ins) // 2
    part = half // chunks
    x = place[0]
    for s, out in enumerate(outs):
        for j in range(half):
            keep = ins[j // part][s, j % part].astype(jnp.float32)
            sent = ins[chunks + j // part][s, j % part].astype(jnp.float32)
            wide[s, pl.ds(j, tok, stride=heads), :] = jnp.where(x == 0, keep, sent)
            wide[s, pl.ds(half + j, tok, stride=heads), :] = jnp.where(x == 0, sent, keep)
        out[...] = wide[s].reshape(tok, heads, width).astype(out.dtype)


def join_heads(place, keeps, sents):
    count, part, tok, width = keeps[0].shape
    heads = 2 * part * len(keeps)
    vmem = pl.BlockSpec(memory_space=pltpu.VMEM)
    return pl.pallas_call(
        functools.partial(join_heads_kernel, count),
        out_shape=(jax.ShapeDtypeStruct((tok, heads, width), jnp.bfloat16),) * count,
        in_specs=[pl.BlockSpec(memory_space=pltpu.SMEM)] + [vmem] * (2 * len(keeps)),
        out_specs=(vmem,) * count,
        scratch_shapes=[pltpu.VMEM((count, tok * heads, width), jnp.float32)],
        compiler_params=pltpu.CompilerParams(vmem_limit_bytes=VMEM_LIMIT),
        name="join_heads",
    )(place, *keeps, *sents)


def body(queries, keys, values, d_out):
    tok = queries.shape[0]
    quad = WINDOW // tok
    assert quad == 4 and lax.axis_size("ctx") % quad == 0
    me = lax.axis_index("ctx")
    x, c, first = (me // 2) % 2, me % 2, (me < quad).astype(jnp.int32)
    place = jnp.stack([x, c, first]).astype(jnp.int32)
    bf, f32 = jnp.bfloat16, jnp.float32
    chunks = 2

    kv_keep, kv_send = split_heads(x, keys, values)
    q_keep, q_send = split_heads(x, queries, d_out)
    kv_x = swap(kv_send, 2)
    kv_1 = shift(kv_keep, quad, wrap=True)
    q_x = swap(q_send, 2)
    kv_2 = shift(kv_x, quad)
    mates = [swap(after(a, kv_1), 1) for a in (kv_keep, kv_x)]
    mates += [swap(kv_1, 1), swap(kv_2, 1)]
    per = kv_keep.shape[1] // chunks

    dq_keep, dq_x, mine, dkv_x = [], [], [], []
    for i in range(chunks):
        keep, send, prev_here, prev_mate, own_here, own_mate = grads(
            i * per, per, place, q_keep, q_x,
            kv_keep, kv_x, mates[0], mates[1], kv_1, kv_2, mates[2], mates[3],
        )
        if i:
            own_mate = after(own_mate, back)
        prev_sum = (prev_here + swap(prev_mate, 1).astype(f32)).astype(bf)
        back = shift(prev_sum, -quad, wrap=i + 1 < chunks)
        own_sum = own_here + swap(own_mate, 1).astype(f32) + back.astype(f32)
        dkv_x.append(swap(own_sum[1].astype(bf), 2))
        mine.append(own_sum[0].astype(bf))
        dq_keep.append(keep[None])
        dq_x.append(swap(after(send, prev_sum), 2)[None])
    (dq,) = join_heads(place, dq_keep, dq_x)
    dk, dv = join_heads(place, mine, dkv_x)
    return dq, dk, dv


def solution(mesh):
    spec = P("ctx", None, None)
    return jax.shard_map(
        body,
        mesh=mesh,
        in_specs=(spec,) * 4,
        out_specs=(spec,) * 3,
        check_vma=False,
    )
```

```python
import functools
import itertools
import math

import jax
import jax.numpy as jnp
from jax import lax
from jax.experimental import pallas as pl
from jax.experimental.pallas import tpu as pltpu
from jax.sharding import PartitionSpec as P

WINDOW = 512
SCORE_SCALE = 168.0 ** -0.5
LOG2E = math.log2(math.e)
NEG = -1e30
VMEM_LIMIT = 48 * 1024 * 1024

NT = (((1,), (1,)), ((), ()))
NN = (((1,), (0,)), ((), ()))


def dot(a, b, dims):
    return lax.dot_general(a, b, dims, preferred_element_type=jnp.float32)


def swap(a, by):
    n = lax.axis_size("ctx")
    return lax.ppermute(a, "ctx", [(i, i ^ by) for i in range(n)])


def shift(a, by, wrap=False):
    n = lax.axis_size("ctx")
    pairs = [(i, (i + by) % n) for i in range(n) if wrap or 0 <= i + by < n]
    return lax.ppermute(a, "ctx", pairs)


def after(a, *others):
    return lax.optimization_barrier((a, *others))[0]


def split_heads(x, a, b):
    both = jnp.stack([a, b]).transpose(0, 2, 1, 3)
    half = a.shape[1] // 2
    return [lax.dynamic_slice_in_dim(both, half * side, half, 1) for side in (x, 1 - x)]


def grads_kernel(
    start, groups, place, keep_q, sent_q, ko, xo, mko, mxo, k1, k2, mk1, mk2, *rest
):
    *done, dq_keep, dq_send, prev_here, prev_mate, own_here, own_mate, kv = rest
    _, all_groups, tok, width = ko.shape
    heads = keep_q.shape[1] // all_groups
    x, c, first = place[0], place[1], place[2]
    blocks = WINDOW // tok
    span = WINDOW + tok
    reach = (2 * blocks - 1) * tok
    mine, other = 2 * x + c, 2 * (1 - x) + c
    mate_mine, mate_other = 2 * x + 1 - c, 2 * (1 - x) + 1 - c
    for ref, slot in (
        (k1, mine), (k2, other), (mk1, mate_mine), (mk2, mate_other),
        (ko, blocks + mine), (xo, blocks + other), (mko, blocks + mate_mine), (mxo, blocks + mate_other),
    ):
        kv[:, :, pl.ds(pl.multiple_of(slot * tok, tok), tok), :] = ref[:, start : start + groups]
    first_head = start * heads if done else 0
    for ref, out in zip(done, (dq_keep, dq_send)):
        out[:first_head] = ref[...]
    rows = pl.ds(pl.multiple_of(c * tok, tok), reach)
    key = lax.broadcasted_iota(jnp.int32, (tok, heads * tok), 0)
    query = lax.broadcasted_iota(jnp.int32, (tok, heads * tok), 1) % tok
    before, upto = key > query, key <= query

    def load(g):
        k, v = kv[0, g, rows, :], kv[1, g, rows, :]
        qs = []
        for xx in range(2):
            pair = []
            for s in range(2):
                mine_of = pl.ds((start + g) * heads, heads)
                keep, sent = keep_q[s, mine_of], sent_q[s, mine_of]
                pair.append(jnp.where(x == xx, keep, sent).reshape(heads * tok, width))
            qs.append(pair)
        return k, v, k.T, qs

    def products(state, xx):
        k, v, kt, qs = state
        q, do = qs[xx]
        win = slice(xx * 2 * tok, xx * 2 * tok + span)
        return dot(k[win], q, NT), dot(v[win], do, NT)

    def weights(state, xx, scores, gp):
        parts = []
        for t in range(blocks + 1):
            part = scores[t * tok : (t + 1) * tok] * (SCORE_SCALE * LOG2E)
            if t < blocks:
                hidden = jnp.logical_and(first == 1, 2 * xx + c + t < blocks)
                part = part + jnp.where(hidden, NEG, 0.0)
            if t == 0:
                part = jnp.where(before, part, NEG)
            if t == blocks:
                part = jnp.where(upto, part, NEG)
            parts.append(part)
        top = jnp.max(functools.reduce(jnp.maximum, parts), axis=0, keepdims=True)
        parts = [jnp.exp2(part - top) for part in parts]
        gps = [gp[t * tok : (t + 1) * tok] for t in range(blocks + 1)]
        total = jnp.sum(sum(parts[1:], parts[0]), axis=0, keepdims=True)
        mixed = [p * g for p, g in zip(parts, gps)]
        inverse = 1.0 / total
        row_dot = jnp.sum(sum(mixed[1:], mixed[0]), axis=0, keepdims=True) * inverse
        parts = [part * inverse for part in parts]
        low = jnp.concatenate([p.astype(jnp.bfloat16) for p in parts], axis=0)
        ds = jnp.concatenate([(p * (g - row_dot)).astype(jnp.bfloat16) for p, g in zip(parts, gps)], axis=0)
        return low, ds

    def outputs(g, state, sides):
        k, v, kt, qs = state
        dqs = []
        for xx in range(2):
            win = slice(xx * 2 * tok, xx * 2 * tok + span)
            dqs.append((dot(kt[:, win], sides[xx][1], NN) * SCORE_SCALE).T.astype(jnp.bfloat16).reshape(heads, tok, width))
        hs = pl.ds(first_head + g * heads, heads)
        dq_keep[hs] = jnp.where(x == 0, dqs[0], dqs[1])
        dq_send[hs] = jnp.where(x == 0, dqs[1], dqs[0])
        cut = span - 2 * tok
        for s, scale in enumerate((SCORE_SCALE, 1.0)):
            w0, w1 = sides[0][1 - s], sides[1][1 - s]
            r0, r1 = qs[0][s], qs[1][s]
            early = dot(w0[: 2 * tok], r0, NN)
            both = dot(w0[2 * tok :], r0, NN) + dot(w1[:cut], r1, NN)
            late = dot(w1[cut:], r1, NN)
            got = jnp.concatenate([early, both, late], axis=0) * scale
            for t in range(0, 2 * blocks - 1, 2):
                ref, xx = (prev_here, t // 2) if t < blocks else (own_here, (t - blocks) // 2)
                ref[xx ^ x, s, g] = got[t * tok : (t + 1) * tok].astype(ref.dtype)
            odd = [got[t * tok : (t + 1) * tok].astype(jnp.bfloat16) for t in (1, 3, 5)]
            zero = jnp.zeros_like(odd[0])
            low_core = c == 0
            four = [
                jnp.where(low_core, odd[0], zero),
                jnp.where(low_core, odd[1], odd[0]),
                jnp.where(low_core, odd[2], odd[1]),
                jnp.where(low_core, zero, odd[2]),
            ]
            for xx in range(2):
                prev_mate[xx ^ x, s, g] = four[xx]
                own_mate[xx ^ x, s, g] = four[2 + xx]

    flow = [(g, xx) for g in range(groups) for xx in range(2)]
    states = {0: load(0)}
    ready = products(states[0], 0)
    sides = {}
    for i, (g, xx) in enumerate(flow):
        now = ready
        if i + 1 < len(flow):
            ng, nx = flow[i + 1]
            if ng not in states:
                states[ng] = load(ng)
            ready = products(states[ng], nx)
        if xx == 0 and g > 0:
            outputs(g - 1, states.pop(g - 1), sides.pop(g - 1))
        sides.setdefault(g, []).append(weights(states[g], xx, *now))
    outputs(groups - 1, states[groups - 1], sides[groups - 1])

def grads(start, groups, done, place, keep_q, sent_q, *kvs):
    _, all_groups, tok, width = kvs[0].shape
    heads = keep_q.shape[1] // all_groups
    bf, f32 = jnp.bfloat16, jnp.float32
    dq_shape = jax.ShapeDtypeStruct(((groups + (start if done else 0)) * heads, tok, width), bf)
    dkv_shape = functools.partial(jax.ShapeDtypeStruct, (2, 2, groups, tok, width))
    vmem = pl.BlockSpec(memory_space=pltpu.VMEM)
    return pl.pallas_call(
        functools.partial(grads_kernel, start, groups),
        out_shape=(dq_shape, dq_shape, dkv_shape(f32), dkv_shape(bf), dkv_shape(f32), dkv_shape(bf)),
        in_specs=[pl.BlockSpec(memory_space=pltpu.SMEM)] + [vmem] * (10 + len(done)),
        out_specs=(vmem,) * 6,
        scratch_shapes=[pltpu.VMEM((2, groups, 2 * WINDOW, width), bf)],
        compiler_params=pltpu.CompilerParams(vmem_limit_bytes=VMEM_LIMIT),
        cost_estimate=pl.CostEstimate(flops=1, bytes_accessed=1, transcendentals=0),
        name="window_grads",
    )(place, keep_q, sent_q, *kvs, *done)


def join_heads_kernel(keeps, sents, count, place, *refs):
    outs, wide = refs[-1 - count : -1], refs[-1]
    refs = refs[: -1 - count][::-1]
    tok, heads, width = outs[0].shape
    half = heads // 2
    x = place[0]

    def total(chunks, s, j):
        part = half // len(chunks)
        terms = [refs[n] for n in chunks[j // part]]
        return sum(r[(s,) * (len(r.shape) - 3) + (j % part,)].astype(jnp.float32) for r in terms)

    for s, out in enumerate(outs):
        for j in range(half):
            keep, sent = total(keeps, s, j), total(sents, s, j)
            wide[s, pl.ds(j, tok, stride=heads), :] = jnp.where(x == 0, keep, sent)
            wide[s, pl.ds(half + j, tok, stride=heads), :] = jnp.where(x == 0, sent, keep)
        out[...] = wide[s].reshape(tok, heads, width).astype(out.dtype)


def join_heads(place, keeps, sents):
    *lead, part, tok, width = keeps[0][0].shape
    count = 2 if lead else 1
    heads = 2 * part * len(keeps)
    numbers = itertools.count()
    number = lambda chunks: [[next(numbers) for _ in terms] for terms in chunks]
    vmem = pl.BlockSpec(memory_space=pltpu.VMEM)
    outs = (jax.ShapeDtypeStruct((tok, heads, width), jnp.bfloat16),) * count
    arrays = [a for terms in keeps + sents for a in terms][::-1]
    got = pl.pallas_call(
        functools.partial(join_heads_kernel, number(keeps), number(sents), count),
        out_shape=outs,
        in_specs=[pl.BlockSpec(memory_space=pltpu.SMEM)] + [vmem] * len(arrays),
        out_specs=(vmem,) * count,
        scratch_shapes=[pltpu.VMEM((count, tok * heads, width), jnp.float32)],
        compiler_params=pltpu.CompilerParams(vmem_limit_bytes=VMEM_LIMIT),
        name="join_heads",
    )(place, *arrays)
    return got if count > 1 else got[0]


def body(queries, keys, values, d_out):
    tok = queries.shape[0]
    quad = WINDOW // tok
    assert quad == 4 and lax.axis_size("ctx") % quad == 0
    me = lax.axis_index("ctx")
    x, c, first = (me // 2) % 2, me % 2, (me < quad).astype(jnp.int32)
    place = jnp.stack([x, c, first]).astype(jnp.int32)
    bf, f32 = jnp.bfloat16, jnp.float32
    chunks = 2

    kv_keep, kv_send = split_heads(x, keys, values)
    q_keep, q_send = split_heads(x, queries, d_out)
    kv_x = swap(kv_send, 2)
    kv_1 = shift(kv_keep, quad, wrap=True)
    q_x = swap(q_send, 2)
    kv_2 = shift(kv_x, quad)
    mates = [swap(after(a, kv_1), 1) for a in (kv_keep, kv_x)]
    mates += [swap(kv_1, 1), swap(kv_2, 1)]
    per = kv_keep.shape[1] // chunks

    sums, parts = [], []
    dq = ()
    for i in range(chunks):
        *dq, prev_here, prev_mate, own_here, own_mate = grads(
            i * per, per, tuple(dq), place, q_keep, q_x,
            kv_keep, kv_x, mates[0], mates[1], kv_1, kv_2, mates[2], mates[3],
        )
        sums.append((prev_here + swap(prev_mate, 1).astype(f32)).astype(bf))
        parts.append(own_here + swap(own_mate, 1).astype(f32))
    dq_x = swap(dq[1], 2)
    back_a = shift(sums[0], -quad, wrap=True)
    back_b2 = shift(sums[1][1], -quad)
    back_b1 = shift(sums[1][0], -quad)
    sum_a = parts[0] + back_a.astype(f32)
    send_a = sum_a[1].astype(bf)
    send_b = (parts[1][1] + after(back_b2, send_a).astype(f32)).astype(bf)
    other_a = swap(send_a, 2)
    other_b = swap(after(send_b, send_a, dq_x), 2)
    dq = join_heads(place, [[dq[0]]], [[after(dq_x, back_b1)]])
    dk, dv = join_heads(
        place, [[sum_a[0].astype(bf)], [parts[1][0], back_b1]], [[other_a], [other_b]]
    )
    return dq, dk, dv


def solution(mesh):
    spec = P("ctx", None, None)
    return jax.shard_map(
        body,
        mesh=mesh,
        in_specs=(spec,) * 4,
        out_specs=(spec,) * 3,
        check_vma=False,
    )
```

```python
import functools
import itertools
import math

import jax
import jax.numpy as jnp
from jax import lax
from jax.experimental import pallas as pl
from jax.experimental.pallas import tpu as pltpu
from jax.sharding import PartitionSpec as P

WINDOW = 512
SCORE_SCALE = 168.0 ** -0.5
LOG2E = math.log2(math.e)
NEG = -1e30
VMEM_LIMIT = 48 * 1024 * 1024

NT = (((1,), (1,)), ((), ()))
NN = (((1,), (0,)), ((), ()))


def dot(a, b, dims):
    return lax.dot_general(a, b, dims, preferred_element_type=jnp.float32)


def swap(a, by):
    n = lax.axis_size("ctx")
    return lax.ppermute(a, "ctx", [(i, i ^ by) for i in range(n)])


def shift(a, by, wrap=False):
    n = lax.axis_size("ctx")
    pairs = [(i, (i + by) % n) for i in range(n) if wrap or 0 <= i + by < n]
    return lax.ppermute(a, "ctx", pairs)


def after(a, *others):
    return lax.optimization_barrier((a, *others))[0]


def split_heads(x, a, b):
    both = jnp.stack([a, b]).transpose(0, 2, 1, 3)
    half = a.shape[1] // 2
    return [lax.dynamic_slice_in_dim(both, half * side, half, 1) for side in (x, 1 - x)]


def grads_kernel(
    start, groups, place, keep_q, sent_q, ko, xo, mko, mxo, k1, k2, mk1, mk2, *rest
):
    *done, dq_keep, dq_send, prev_here, prev_mate, own_here, own_mate, kv = rest
    _, all_groups, tok, width = ko.shape
    heads = keep_q.shape[1] // all_groups
    x, c, first = place[0], place[1], place[2]
    blocks = WINDOW // tok
    span = WINDOW + tok
    reach = (2 * blocks - 1) * tok
    mine, other = 2 * x + c, 2 * (1 - x) + c
    mate_mine, mate_other = 2 * x + 1 - c, 2 * (1 - x) + 1 - c
    for ref, slot in (
        (k1, mine), (k2, other), (mk1, mate_mine), (mk2, mate_other),
        (ko, blocks + mine), (xo, blocks + other), (mko, blocks + mate_mine), (mxo, blocks + mate_other),
    ):
        kv[:, :, pl.ds(pl.multiple_of(slot * tok, tok), tok), :] = ref[:, start : start + groups]
    first_head = start * heads if done else 0
    for ref, out in zip(done, (dq_keep, dq_send)):
        out[:first_head] = ref[...]
    rows = pl.ds(pl.multiple_of(c * tok, tok), reach)
    key = lax.broadcasted_iota(jnp.int32, (tok, heads * tok), 0)
    query = lax.broadcasted_iota(jnp.int32, (tok, heads * tok), 1) % tok
    before, upto = key > query, key <= query

    def load(g):
        k, v = kv[0, g, rows, :], kv[1, g, rows, :]
        qs = []
        for xx in range(2):
            pair = []
            for s in range(2):
                mine_of = pl.ds((start + g) * heads, heads)
                keep, sent = keep_q[s, mine_of], sent_q[s, mine_of]
                pair.append(jnp.where(x == xx, keep, sent).reshape(heads * tok, width))
            qs.append(pair)
        return k, v, k.T, qs

    def products(state, xx):
        k, v, kt, qs = state
        q, do = qs[xx]
        win = slice(xx * 2 * tok, xx * 2 * tok + span)
        return dot(k[win], q, NT), dot(v[win], do, NT)

    def weights(state, xx, scores, gp):
        parts = []
        for t in range(blocks + 1):
            part = scores[t * tok : (t + 1) * tok] * (SCORE_SCALE * LOG2E)
            if t < blocks:
                hidden = jnp.logical_and(first == 1, 2 * xx + c + t < blocks)
                part = part + jnp.where(hidden, NEG, 0.0)
            if t == 0:
                part = jnp.where(before, part, NEG)
            if t == blocks:
                part = jnp.where(upto, part, NEG)
            parts.append(part)
        top = jnp.max(functools.reduce(jnp.maximum, parts), axis=0, keepdims=True)
        parts = [jnp.exp2(part - top) for part in parts]
        gps = [gp[t * tok : (t + 1) * tok] for t in range(blocks + 1)]
        total = jnp.sum(sum(parts[1:], parts[0]), axis=0, keepdims=True)
        mixed = [p * g for p, g in zip(parts, gps)]
        inverse = 1.0 / total
        row_dot = jnp.sum(sum(mixed[1:], mixed[0]), axis=0, keepdims=True) * inverse
        parts = [part * inverse for part in parts]
        low = jnp.concatenate([p.astype(jnp.bfloat16) for p in parts], axis=0)
        ds = jnp.concatenate([(p * (g - row_dot)).astype(jnp.bfloat16) for p, g in zip(parts, gps)], axis=0)
        return low, ds

    def outputs(g, state, sides):
        k, v, kt, qs = state
        dqs = []
        for xx in range(2):
            win = slice(xx * 2 * tok, xx * 2 * tok + span)
            dqs.append((dot(kt[:, win], sides[xx][1], NN) * SCORE_SCALE).T.astype(jnp.bfloat16).reshape(heads, tok, width))
        hs = pl.ds(first_head + g * heads, heads)
        dq_keep[hs] = jnp.where(x == 0, dqs[0], dqs[1])
        dq_send[hs] = jnp.where(x == 0, dqs[1], dqs[0])
        cut = span - 2 * tok
        for s, scale in enumerate((SCORE_SCALE, 1.0)):
            w0, w1 = sides[0][1 - s], sides[1][1 - s]
            r0, r1 = qs[0][s], qs[1][s]
            early = dot(w0[: 2 * tok], r0, NN)
            both = dot(w0[2 * tok :], r0, NN) + dot(w1[:cut], r1, NN)
            late = dot(w1[cut:], r1, NN)
            got = jnp.concatenate([early, both, late], axis=0) * scale
            for t in range(0, 2 * blocks - 1, 2):
                ref, xx = (prev_here, t // 2) if t < blocks else (own_here, (t - blocks) // 2)
                ref[xx ^ x, s, g] = got[t * tok : (t + 1) * tok].astype(ref.dtype)
            odd = [got[t * tok : (t + 1) * tok].astype(jnp.bfloat16) for t in (1, 3, 5)]
            zero = jnp.zeros_like(odd[0])
            low_core = c == 0
            four = [
                jnp.where(low_core, odd[0], zero),
                jnp.where(low_core, odd[1], odd[0]),
                jnp.where(low_core, odd[2], odd[1]),
                jnp.where(low_core, zero, odd[2]),
            ]
            for xx in range(2):
                prev_mate[xx ^ x, s, g] = four[xx]
                own_mate[xx ^ x, s, g] = four[2 + xx]

    flow = [(g, xx) for g in range(groups) for xx in range(2)]
    states = {0: load(0)}
    ready = products(states[0], 0)
    sides = {}
    for i, (g, xx) in enumerate(flow):
        now = ready
        if i + 1 < len(flow):
            ng, nx = flow[i + 1]
            if ng not in states:
                states[ng] = load(ng)
            ready = products(states[ng], nx)
        if xx == 0 and g > 0:
            outputs(g - 1, states.pop(g - 1), sides.pop(g - 1))
        sides.setdefault(g, []).append(weights(states[g], xx, *now))
    outputs(groups - 1, states[groups - 1], sides[groups - 1])

def grads(start, groups, done, place, keep_q, sent_q, *kvs):
    _, all_groups, tok, width = kvs[0].shape
    heads = keep_q.shape[1] // all_groups
    bf, f32 = jnp.bfloat16, jnp.float32
    dq_shape = jax.ShapeDtypeStruct(((groups + (start if done else 0)) * heads, tok, width), bf)
    dkv_shape = functools.partial(jax.ShapeDtypeStruct, (2, 2, groups, tok, width))
    vmem = pl.BlockSpec(memory_space=pltpu.VMEM)
    return pl.pallas_call(
        functools.partial(grads_kernel, start, groups),
        out_shape=(dq_shape, dq_shape, dkv_shape(f32), dkv_shape(bf), dkv_shape(f32), dkv_shape(bf)),
        in_specs=[pl.BlockSpec(memory_space=pltpu.SMEM)] + [vmem] * (10 + len(done)),
        out_specs=(vmem,) * 6,
        scratch_shapes=[pltpu.VMEM((2, groups, 2 * WINDOW, width), bf)],
        compiler_params=pltpu.CompilerParams(vmem_limit_bytes=VMEM_LIMIT),
        cost_estimate=pl.CostEstimate(flops=1, bytes_accessed=1, transcendentals=0),
        name="window_grads",
    )(place, keep_q, sent_q, *kvs, *done)


def join_heads_kernel(keeps, sents, count, place, *refs):
    outs, wide = refs[-1 - count : -1], refs[-1]
    refs = refs[: -1 - count][::-1]
    tok, heads, width = outs[0].shape
    half = heads // 2
    x = place[0]

    def total(chunks, s, j):
        part = half // len(chunks)
        terms = [refs[n] for n in chunks[j // part]]
        return sum(r[(s,) * (len(r.shape) - 3) + (j % part,)].astype(jnp.float32) for r in terms)

    for s, out in enumerate(outs):
        for j in range(half):
            keep, sent = total(keeps, s, j), total(sents, s, j)
            wide[s, pl.ds(j, tok, stride=heads), :] = jnp.where(x == 0, keep, sent)
            wide[s, pl.ds(half + j, tok, stride=heads), :] = jnp.where(x == 0, sent, keep)
        out[...] = wide[s].reshape(tok, heads, width).astype(out.dtype)


def join_heads(place, keeps, sents):
    *lead, part, tok, width = keeps[0][0].shape
    count = 2 if lead else 1
    heads = 2 * part * len(keeps)
    numbers = itertools.count()
    number = lambda chunks: [[next(numbers) for _ in terms] for terms in chunks]
    vmem = pl.BlockSpec(memory_space=pltpu.VMEM)
    outs = (jax.ShapeDtypeStruct((tok, heads, width), jnp.bfloat16),) * count
    arrays = [a for terms in keeps + sents for a in terms][::-1]
    got = pl.pallas_call(
        functools.partial(join_heads_kernel, number(keeps), number(sents), count),
        out_shape=outs,
        in_specs=[pl.BlockSpec(memory_space=pltpu.SMEM)] + [vmem] * len(arrays),
        out_specs=(vmem,) * count,
        scratch_shapes=[pltpu.VMEM((count, tok * heads, width), jnp.float32)],
        compiler_params=pltpu.CompilerParams(vmem_limit_bytes=VMEM_LIMIT),
        name="join_heads",
    )(place, *arrays)
    return got if count > 1 else got[0]


def body(queries, keys, values, d_out):
    tok = queries.shape[0]
    quad = WINDOW // tok
    assert quad == 4 and lax.axis_size("ctx") % quad == 0
    me = lax.axis_index("ctx")
    x, c, first = (me // 2) % 2, me % 2, (me < quad).astype(jnp.int32)
    place = jnp.stack([x, c, first]).astype(jnp.int32)
    bf, f32 = jnp.bfloat16, jnp.float32
    chunks = 2

    kv_keep, kv_send = split_heads(x, keys, values)
    q_keep, q_send = split_heads(x, queries, d_out)
    kv_x = swap(kv_send, 2)
    kv_1 = shift(kv_keep, quad, wrap=True)
    q_x = swap(q_send, 2)
    kv_2 = shift(kv_x, quad)
    mates = [swap(after(a, kv_1), 1) for a in (kv_keep, kv_x)]
    mates += [swap(kv_1, 1), swap(kv_2, 1)]
    per = kv_keep.shape[1] // chunks

    sums, parts = [], []
    dq = ()
    for i in range(chunks):
        *dq, prev_here, prev_mate, own_here, own_mate = grads(
            i * per, per, tuple(dq), place, q_keep, q_x,
            kv_keep, kv_x, mates[0], mates[1], kv_1, kv_2, mates[2], mates[3],
        )
        sums.append((prev_here + swap(prev_mate, 1).astype(f32)).astype(bf))
        parts.append((own_here, own_mate))
    parts = [here + swap(after(mate, sums[0]), 1).astype(f32) for here, mate in parts]
    dq_x = swap(after(dq[1], sums[0]), 2)
    back_a = shift(sums[0], -quad)
    back_b2 = shift(sums[1][1], -quad)
    back_b1 = shift(sums[1][0], -quad)
    sum_a = parts[0] + back_a.astype(f32)
    send_a = sum_a[1].astype(bf)
    send_b = (parts[1][1] + after(back_b2, send_a).astype(f32)).astype(bf)
    other_a = swap(after(send_a, dq_x), 2)
    other_b = swap(after(send_b, send_a), 2)
    dq = join_heads(place, [[dq[0]]], [[after(dq_x, back_b1)]])
    dk, dv = join_heads(
        place, [[sum_a[0].astype(bf)], [parts[1][0], back_b1]], [[other_a], [other_b]]
    )
    return dq, dk, dv


def solution(mesh):
    spec = P("ctx", None, None)
    return jax.shard_map(
        body,
        mesh=mesh,
        in_specs=(spec,) * 4,
        out_specs=(spec,) * 3,
        check_vma=False,
    )
```

```python
import functools
import itertools
import math

import jax
import jax.numpy as jnp
from jax import lax
from jax.experimental import pallas as pl
from jax.experimental.pallas import tpu as pltpu
from jax.sharding import PartitionSpec as P

WINDOW = 512
SCORE_SCALE = 168.0 ** -0.5
LOG2E = math.log2(math.e)
NEG = -1e30
VMEM_LIMIT = 48 * 1024 * 1024
PIECES = 2

NT = (((1,), (1,)), ((), ()))
NN = (((1,), (0,)), ((), ()))


def dot(a, b, dims):
    return lax.dot_general(a, b, dims, preferred_element_type=jnp.float32)


def swap(a, by):
    n = lax.axis_size("ctx")
    return lax.ppermute(a, "ctx", [(i, i ^ by) for i in range(n)])


def shift(a, by, wrap=False):
    n = lax.axis_size("ctx")
    pairs = [(i, (i + by) % n) for i in range(n) if wrap or 0 <= i + by < n]
    return lax.ppermute(a, "ctx", pairs)


def after(a, *others):
    return lax.optimization_barrier((a, *others))[0]


def split_heads(x, a, b):
    both = jnp.stack([a, b]).transpose(0, 2, 1, 3)
    half = a.shape[1] // 2
    return [lax.dynamic_slice_in_dim(both, half * side, half, 1) for side in (x, 1 - x)]


def grads_kernel(
    start, groups, place, keep_q, sent_q, ko, xo, mko, mxo, k1, k2, mk1, mk2, *rest
):
    *done, dq_keep, dq_send, prev_here, prev_mate, own_here, own_mate, kv = rest
    _, all_groups, tok, width = ko.shape
    heads = keep_q.shape[1] // all_groups
    x, c, first = place[0], place[1], place[2]
    blocks = WINDOW // tok
    span = WINDOW + tok
    reach = (2 * blocks - 1) * tok
    mine, other = 2 * x + c, 2 * (1 - x) + c
    mate_mine, mate_other = 2 * x + 1 - c, 2 * (1 - x) + 1 - c
    for ref, slot in (
        (k1, mine), (k2, other), (mk1, mate_mine), (mk2, mate_other),
        (ko, blocks + mine), (xo, blocks + other), (mko, blocks + mate_mine), (mxo, blocks + mate_other),
    ):
        kv[:, :, pl.ds(pl.multiple_of(slot * tok, tok), tok), :] = ref[:, start : start + groups]
    first_head = start * heads if done else 0
    for ref, out in zip(done, (dq_keep, dq_send)):
        out[:first_head] = ref[...]
    rows = pl.ds(pl.multiple_of(c * tok, tok), reach)
    key = lax.broadcasted_iota(jnp.int32, (tok, heads * tok), 0)
    query = lax.broadcasted_iota(jnp.int32, (tok, heads * tok), 1) % tok
    before, upto = key > query, key <= query

    def load(g):
        k, v = kv[0, g, rows, :], kv[1, g, rows, :]
        qs = []
        for xx in range(2):
            pair = []
            for s in range(2):
                mine_of = pl.ds((start + g) * heads, heads)
                keep, sent = keep_q[s, mine_of], sent_q[s, mine_of]
                pair.append(jnp.where(x == xx, keep, sent).reshape(heads * tok, width))
            qs.append(pair)
        return k, v, k.T, qs

    def products(state, xx):
        k, v, kt, qs = state
        q, do = qs[xx]
        win = slice(xx * 2 * tok, xx * 2 * tok + span)
        return dot(k[win], q, NT), dot(v[win], do, NT)

    def weights(state, xx, scores, gp):
        parts = []
        for t in range(blocks + 1):
            part = scores[t * tok : (t + 1) * tok] * (SCORE_SCALE * LOG2E)
            if t < blocks:
                hidden = jnp.logical_and(first == 1, 2 * xx + c + t < blocks)
                part = part + jnp.where(hidden, NEG, 0.0)
            if t == 0:
                part = jnp.where(before, part, NEG)
            if t == blocks:
                part = jnp.where(upto, part, NEG)
            parts.append(part)
        top = jnp.max(functools.reduce(jnp.maximum, parts), axis=0, keepdims=True)
        parts = [jnp.exp2(part - top) for part in parts]
        gps = [gp[t * tok : (t + 1) * tok] for t in range(blocks + 1)]
        total = jnp.sum(sum(parts[1:], parts[0]), axis=0, keepdims=True)
        mixed = [p * g for p, g in zip(parts, gps)]
        inverse = 1.0 / total
        row_dot = jnp.sum(sum(mixed[1:], mixed[0]), axis=0, keepdims=True) * inverse
        parts = [part * inverse for part in parts]
        low = jnp.concatenate([p.astype(jnp.bfloat16) for p in parts], axis=0)
        ds = jnp.concatenate([(p * (g - row_dot)).astype(jnp.bfloat16) for p, g in zip(parts, gps)], axis=0)
        return low, ds

    def outputs(g, state, sides):
        k, v, kt, qs = state
        dqs = []
        for xx in range(2):
            win = slice(xx * 2 * tok, xx * 2 * tok + span)
            dqs.append((dot(kt[:, win], sides[xx][1], NN) * SCORE_SCALE).T.astype(jnp.bfloat16).reshape(heads, tok, width))
        hs = pl.ds(first_head + g * heads, heads)
        dq_keep[hs] = jnp.where(x == 0, dqs[0], dqs[1])
        dq_send[hs] = jnp.where(x == 0, dqs[1], dqs[0])
        cut = span - 2 * tok
        for s, scale in enumerate((SCORE_SCALE, 1.0)):
            w0, w1 = sides[0][1 - s], sides[1][1 - s]
            r0, r1 = qs[0][s], qs[1][s]
            early = dot(w0[: 2 * tok], r0, NN)
            both = dot(w0[2 * tok :], r0, NN) + dot(w1[:cut], r1, NN)
            late = dot(w1[cut:], r1, NN)
            got = jnp.concatenate([early, both, late], axis=0) * scale
            for t in range(0, 2 * blocks - 1, 2):
                ref, xx = (prev_here, t // 2) if t < blocks else (own_here, (t - blocks) // 2)
                ref[xx ^ x, s, g] = got[t * tok : (t + 1) * tok].astype(ref.dtype)
            odd = [got[t * tok : (t + 1) * tok].astype(jnp.bfloat16) for t in (1, 3, 5)]
            zero = jnp.zeros_like(odd[0])
            low_core = c == 0
            four = [
                jnp.where(low_core, odd[0], zero),
                jnp.where(low_core, odd[1], odd[0]),
                jnp.where(low_core, odd[2], odd[1]),
                jnp.where(low_core, zero, odd[2]),
            ]
            for xx in range(2):
                prev_mate[xx ^ x, s, g] = four[xx]
                own_mate[xx ^ x, s, g] = four[2 + xx]

    flow = [(g, xx) for g in range(groups) for xx in range(2)]
    states = {0: load(0)}
    ready = products(states[0], 0)
    sides = {}
    for i, (g, xx) in enumerate(flow):
        now = ready
        if i + 1 < len(flow):
            ng, nx = flow[i + 1]
            if ng not in states:
                states[ng] = load(ng)
            ready = products(states[ng], nx)
        if xx == 0 and g > 0:
            outputs(g - 1, states.pop(g - 1), sides.pop(g - 1))
        sides.setdefault(g, []).append(weights(states[g], xx, *now))
    outputs(groups - 1, states[groups - 1], sides[groups - 1])

def grads(start, groups, done, place, keep_q, sent_q, *kvs):
    _, all_groups, tok, width = kvs[0].shape
    heads = keep_q.shape[1] // all_groups
    bf, f32 = jnp.bfloat16, jnp.float32
    dq_shape = jax.ShapeDtypeStruct(((groups + (start if done else 0)) * heads, tok, width), bf)
    dkv_shape = functools.partial(jax.ShapeDtypeStruct, (2, 2, groups, tok, width))
    vmem = pl.BlockSpec(memory_space=pltpu.VMEM)
    return pl.pallas_call(
        functools.partial(grads_kernel, start, groups),
        out_shape=(dq_shape, dq_shape, dkv_shape(f32), dkv_shape(bf), dkv_shape(f32), dkv_shape(bf)),
        in_specs=[pl.BlockSpec(memory_space=pltpu.SMEM)] + [vmem] * (10 + len(done)),
        out_specs=(vmem,) * 6,
        scratch_shapes=[pltpu.VMEM((2, groups, 2 * WINDOW, width), bf)],
        compiler_params=pltpu.CompilerParams(vmem_limit_bytes=VMEM_LIMIT),
        cost_estimate=pl.CostEstimate(flops=1, bytes_accessed=1, transcendentals=0),
        name="window_grads",
    )(place, keep_q, sent_q, *kvs, *done)


def join_heads_kernel(keeps, sents, count, place, *refs):
    *refs, wide, ready, sems = refs
    outs, refs = refs[-count:], refs[:-count][::-1]
    tok, heads, width = outs[0].shape
    half = heads // 2
    rows = tok // PIECES
    x = place[0]

    def total(chunks, s, j, at):
        part = half // len(chunks)
        terms = [refs[n] for n in chunks[j // part]]
        return sum(r[(s,) * (len(r.shape) - 3) + (j % part, at)].astype(jnp.float32) for r in terms)

    copies = []
    for s, out in enumerate(outs):
        for piece in range(PIECES):
            at = pl.ds(piece * rows, rows)
            n = s * PIECES + piece
            for j in range(half):
                keep, sent = total(keeps, s, j, at), total(sents, s, j, at)
                wide[n, pl.ds(j, rows, stride=heads), :] = jnp.where(x == 0, keep, sent)
                wide[n, pl.ds(half + j, rows, stride=heads), :] = jnp.where(x == 0, sent, keep)
            ready[n] = wide[n].reshape(rows, heads, width).astype(out.dtype)
            copies.append(pltpu.make_async_copy(ready.at[n], out.at[at], sems.at[n]))
            copies[-1].start()
    for copy in copies:
        copy.wait()


def join_heads(place, keeps, sents):
    *lead, part, tok, width = keeps[0][0].shape
    count = 2 if lead else 1
    heads = 2 * part * len(keeps)
    numbers = itertools.count()
    number = lambda chunks: [[next(numbers) for _ in terms] for terms in chunks]
    vmem = pl.BlockSpec(memory_space=pltpu.VMEM)
    outs = (jax.ShapeDtypeStruct((tok, heads, width), jnp.bfloat16),) * count
    arrays = [a for terms in keeps + sents for a in terms][::-1]
    got = pl.pallas_call(
        functools.partial(join_heads_kernel, number(keeps), number(sents), count),
        out_shape=outs,
        in_specs=[pl.BlockSpec(memory_space=pltpu.SMEM)] + [vmem] * len(arrays),
        out_specs=(pl.BlockSpec(memory_space=pl.ANY),) * count,
        scratch_shapes=[
            pltpu.VMEM((count * PIECES, tok // PIECES * heads, width), jnp.float32),
            pltpu.VMEM((count * PIECES, tok // PIECES, heads, width), jnp.bfloat16),
            pltpu.SemaphoreType.DMA((count * PIECES,)),
        ],
        compiler_params=pltpu.CompilerParams(vmem_limit_bytes=VMEM_LIMIT),
        name="join_heads",
    )(place, *arrays)
    return got if count > 1 else got[0]


def body(queries, keys, values, d_out):
    tok = queries.shape[0]
    quad = WINDOW // tok
    assert quad == 4 and lax.axis_size("ctx") % quad == 0
    me = lax.axis_index("ctx")
    x, c, first = (me // 2) % 2, me % 2, (me < quad).astype(jnp.int32)
    place = jnp.stack([x, c, first]).astype(jnp.int32)
    bf, f32 = jnp.bfloat16, jnp.float32
    chunks = 2

    kv_keep, kv_send = split_heads(x, keys, values)
    q_keep, q_send = split_heads(x, queries, d_out)
    kv_x = swap(kv_send, 2)
    kv_1 = shift(kv_keep, quad, wrap=True)
    q_x = swap(q_send, 2)
    kv_2 = shift(kv_x, quad)
    mates = [swap(after(a, kv_1), 1) for a in (kv_keep, kv_x)]
    mates += [swap(kv_1, 1), swap(kv_2, 1)]
    per = kv_keep.shape[1] // chunks

    sums, parts = [], []
    dq = ()
    for i in range(chunks):
        *dq, prev_here, prev_mate, own_here, own_mate = grads(
            i * per, per, tuple(dq), place, q_keep, q_x,
            kv_keep, kv_x, mates[0], mates[1], kv_1, kv_2, mates[2], mates[3],
        )
        sums.append((prev_here + swap(prev_mate, 1).astype(f32)).astype(bf))
        parts.append((own_here, own_mate))
    parts = [here + swap(after(mate, sums[0]), 1).astype(f32) for here, mate in parts]
    dq_x = swap(after(dq[1], sums[0]), 2)
    back_a = shift(sums[0], -quad)
    back_b2 = shift(sums[1][1], -quad)
    back_b1 = shift(sums[1][0], -quad)
    sum_a = parts[0] + back_a.astype(f32)
    send_a = sum_a[1].astype(bf)
    send_b = (parts[1][1] + after(back_b2, send_a).astype(f32)).astype(bf)
    other_a = swap(after(send_a, dq_x), 2)
    other_b = swap(after(send_b, send_a), 2)
    dq = join_heads(place, [[dq[0]]], [[after(dq_x, back_b1)]])
    dk, dv = join_heads(
        place, [[sum_a[0].astype(bf)], [parts[1][0], back_b1]], [[other_a], [other_b]]
    )
    return dq, dk, dv


def solution(mesh):
    spec = P("ctx", None, None)
    return jax.shard_map(
        body,
        mesh=mesh,
        in_specs=(spec,) * 4,
        out_specs=(spec,) * 3,
        check_vma=False,
    )
```

```python
import functools
import itertools
import math

import jax
import jax.numpy as jnp
from jax import lax
from jax.experimental import pallas as pl
from jax.experimental.pallas import tpu as pltpu
from jax.sharding import PartitionSpec as P

WINDOW = 512
SCORE_SCALE = 168.0 ** -0.5
LOG2E = math.log2(math.e)
NEG = -1e30
VMEM_LIMIT = 48 * 1024 * 1024

NT = (((1,), (1,)), ((), ()))
NN = (((1,), (0,)), ((), ()))


def dot(a, b, dims):
    return lax.dot_general(a, b, dims, preferred_element_type=jnp.float32)


def swap(a, by):
    n = lax.axis_size("ctx")
    return lax.ppermute(a, "ctx", [(i, i ^ by) for i in range(n)])


def shift(a, by, wrap=False):
    n = lax.axis_size("ctx")
    pairs = [(i, (i + by) % n) for i in range(n) if wrap or 0 <= i + by < n]
    return lax.ppermute(a, "ctx", pairs)


def after(a, *others):
    return lax.optimization_barrier((a, *others))[0]


def split_heads(x, a, b):
    both = jnp.stack([a, b]).transpose(0, 2, 1, 3)
    half = a.shape[1] // 2
    return [lax.dynamic_slice_in_dim(both, half * side, half, 1) for side in (x, 1 - x)]


def grads_kernel(
    start, groups, place, keep_q, sent_q, ko, xo, mko, mxo, k1, k2, mk1, mk2, *rest
):
    *done, dq_keep, dq_send, prev_here, prev_mate, own_here, own_mate, kv = rest
    _, all_groups, tok, width = ko.shape
    heads = keep_q.shape[1] // all_groups
    x, c, first = place[0], place[1], place[2]
    blocks = WINDOW // tok
    span = WINDOW + tok
    reach = (2 * blocks - 1) * tok
    mine, other = 2 * x + c, 2 * (1 - x) + c
    mate_mine, mate_other = 2 * x + 1 - c, 2 * (1 - x) + 1 - c
    for ref, slot in (
        (k1, mine), (k2, other), (mk1, mate_mine), (mk2, mate_other),
        (ko, blocks + mine), (xo, blocks + other), (mko, blocks + mate_mine), (mxo, blocks + mate_other),
    ):
        kv[:, :, pl.ds(pl.multiple_of(slot * tok, tok), tok), :] = ref[:, start : start + groups]
    first_head = start * heads if done else 0
    for ref, out in zip(done, (dq_keep, dq_send)):
        out[:first_head] = ref[...]
    rows = pl.ds(pl.multiple_of(c * tok, tok), reach)
    key = lax.broadcasted_iota(jnp.int32, (tok, heads * tok), 0)
    query = lax.broadcasted_iota(jnp.int32, (tok, heads * tok), 1) % tok
    before, upto = key > query, key <= query

    def load(g):
        k, v = kv[0, g, rows, :], kv[1, g, rows, :]
        qs = []
        for xx in range(2):
            pair = []
            for s in range(2):
                mine_of = pl.ds((start + g) * heads, heads)
                keep, sent = keep_q[s, mine_of], sent_q[s, mine_of]
                pair.append(jnp.where(x == xx, keep, sent).reshape(heads * tok, width))
            qs.append(pair)
        return k, v, k.T, qs

    def products(state, xx):
        k, v, kt, qs = state
        q, do = qs[xx]
        win = slice(xx * 2 * tok, xx * 2 * tok + span)
        return dot(k[win], q, NT), dot(v[win], do, NT)

    def weights(state, xx, scores, gp):
        parts = []
        for t in range(blocks + 1):
            part = scores[t * tok : (t + 1) * tok] * (SCORE_SCALE * LOG2E)
            if t < blocks:
                hidden = jnp.logical_and(first == 1, 2 * xx + c + t < blocks)
                part = part + jnp.where(hidden, NEG, 0.0)
            if t == 0:
                part = jnp.where(before, part, NEG)
            if t == blocks:
                part = jnp.where(upto, part, NEG)
            parts.append(part)
        top = jnp.max(functools.reduce(jnp.maximum, parts), axis=0, keepdims=True)
        parts = [jnp.exp2(part - top) for part in parts]
        gps = [gp[t * tok : (t + 1) * tok] for t in range(blocks + 1)]
        total = jnp.sum(sum(parts[1:], parts[0]), axis=0, keepdims=True)
        mixed = [p * g for p, g in zip(parts, gps)]
        inverse = 1.0 / total
        row_dot = jnp.sum(sum(mixed[1:], mixed[0]), axis=0, keepdims=True) * inverse
        parts = [part * inverse for part in parts]
        low = jnp.concatenate([p.astype(jnp.bfloat16) for p in parts], axis=0)
        ds = jnp.concatenate([(p * (g - row_dot)).astype(jnp.bfloat16) for p, g in zip(parts, gps)], axis=0)
        return low, ds

    def outputs(g, state, sides):
        k, v, kt, qs = state
        dqs = []
        for xx in range(2):
            win = slice(xx * 2 * tok, xx * 2 * tok + span)
            dqs.append((dot(kt[:, win], sides[xx][1], NN) * SCORE_SCALE).T.astype(jnp.bfloat16).reshape(heads, tok, width))
        hs = pl.ds(first_head + g * heads, heads)
        dq_keep[hs] = jnp.where(x == 0, dqs[0], dqs[1])
        dq_send[hs] = jnp.where(x == 0, dqs[1], dqs[0])
        cut = span - 2 * tok
        for s, scale in enumerate((SCORE_SCALE, 1.0)):
            w0, w1 = sides[0][1 - s], sides[1][1 - s]
            r0, r1 = qs[0][s], qs[1][s]
            early = dot(w0[: 2 * tok], r0, NN)
            both = dot(w0[2 * tok :], r0, NN) + dot(w1[:cut], r1, NN)
            late = dot(w1[cut:], r1, NN)
            got = jnp.concatenate([early, both, late], axis=0) * scale
            for t in range(0, 2 * blocks - 1, 2):
                ref, xx = (prev_here, t // 2) if t < blocks else (own_here, (t - blocks) // 2)
                ref[xx ^ x, s, g] = got[t * tok : (t + 1) * tok].astype(ref.dtype)
            odd = [got[t * tok : (t + 1) * tok].astype(jnp.bfloat16) for t in (1, 3, 5)]
            zero = jnp.zeros_like(odd[0])
            low_core = c == 0
            four = [
                jnp.where(low_core, odd[0], zero),
                jnp.where(low_core, odd[1], odd[0]),
                jnp.where(low_core, odd[2], odd[1]),
                jnp.where(low_core, zero, odd[2]),
            ]
            for xx in range(2):
                prev_mate[xx ^ x, s, g] = four[xx]
                own_mate[xx ^ x, s, g] = four[2 + xx]

    flow = [(g, xx) for g in range(groups) for xx in range(2)]
    states = {0: load(0)}
    ready = products(states[0], 0)
    sides = {}
    for i, (g, xx) in enumerate(flow):
        now = ready
        if i + 1 < len(flow):
            ng, nx = flow[i + 1]
            if ng not in states:
                states[ng] = load(ng)
            ready = products(states[ng], nx)
        if xx == 0 and g > 0:
            outputs(g - 1, states.pop(g - 1), sides.pop(g - 1))
        sides.setdefault(g, []).append(weights(states[g], xx, *now))
    outputs(groups - 1, states[groups - 1], sides[groups - 1])

def grads(start, groups, done, place, keep_q, sent_q, *kvs):
    _, all_groups, tok, width = kvs[0].shape
    heads = keep_q.shape[1] // all_groups
    bf, f32 = jnp.bfloat16, jnp.float32
    dq_shape = jax.ShapeDtypeStruct(((groups + (start if done else 0)) * heads, tok, width), bf)
    dkv_shape = functools.partial(jax.ShapeDtypeStruct, (2, 2, groups, tok, width))
    vmem = pl.BlockSpec(memory_space=pltpu.VMEM)
    return pl.pallas_call(
        functools.partial(grads_kernel, start, groups),
        out_shape=(dq_shape, dq_shape, dkv_shape(f32), dkv_shape(bf), dkv_shape(f32), dkv_shape(bf)),
        in_specs=[pl.BlockSpec(memory_space=pltpu.SMEM)] + [vmem] * (10 + len(done)),
        out_specs=(vmem,) * 6,
        scratch_shapes=[pltpu.VMEM((2, groups, 2 * WINDOW, width), bf)],
        compiler_params=pltpu.CompilerParams(vmem_limit_bytes=VMEM_LIMIT),
        cost_estimate=pl.CostEstimate(flops=1, bytes_accessed=1, transcendentals=0),
        name="window_grads",
    )(place, keep_q, sent_q, *kvs, *done)


def join_heads_kernel(keeps, sents, count, place, *refs):
    outs, wide = refs[-1 - count : -1], refs[-1]
    refs = refs[: -1 - count][::-1]
    tok, heads, width = outs[0].shape
    half = heads // 2
    x = place[0]

    def total(chunks, s, j):
        part = half // len(chunks)
        terms = [refs[n] for n in chunks[j // part]]
        return sum(r[(s,) * (len(r.shape) - 3) + (j % part,)].astype(jnp.float32) for r in terms)

    for s, out in enumerate(outs):
        for j in range(half):
            keep, sent = total(keeps, s, j), total(sents, s, j)
            wide[s, pl.ds(j, tok, stride=heads), :] = jnp.where(x == 0, keep, sent)
            wide[s, pl.ds(half + j, tok, stride=heads), :] = jnp.where(x == 0, sent, keep)
        out[...] = wide[s].reshape(tok, heads, width).astype(out.dtype)


def join_heads(place, keeps, sents):
    *lead, part, tok, width = keeps[0][0].shape
    count = 2 if lead else 1
    heads = 2 * part * len(keeps)
    numbers = itertools.count()
    number = lambda chunks: [[next(numbers) for _ in terms] for terms in chunks]
    vmem = pl.BlockSpec(memory_space=pltpu.VMEM)
    outs = (jax.ShapeDtypeStruct((tok, heads, width), jnp.bfloat16),) * count
    arrays = [a for terms in keeps + sents for a in terms][::-1]
    got = pl.pallas_call(
        functools.partial(join_heads_kernel, number(keeps), number(sents), count),
        out_shape=outs,
        in_specs=[pl.BlockSpec(memory_space=pltpu.SMEM)] + [vmem] * len(arrays),
        out_specs=(vmem,) * count,
        scratch_shapes=[pltpu.VMEM((count, tok * heads, width), jnp.float32)],
        compiler_params=pltpu.CompilerParams(vmem_limit_bytes=VMEM_LIMIT),
        name="join_heads",
    )(place, *arrays)
    return got if count > 1 else got[0]


def body(queries, keys, values, d_out):
    tok = queries.shape[0]
    quad = WINDOW // tok
    assert quad == 4 and lax.axis_size("ctx") % quad == 0
    me = lax.axis_index("ctx")
    x, c, first = (me // 2) % 2, me % 2, (me < quad).astype(jnp.int32)
    place = jnp.stack([x, c, first]).astype(jnp.int32)
    bf, f32 = jnp.bfloat16, jnp.float32
    chunks = 2

    kv_keep, kv_send = split_heads(x, keys, values)
    q_keep, q_send = split_heads(x, queries, d_out)
    kv_x = swap(kv_send, 2)
    kv_1 = shift(kv_keep, quad)
    q_x = swap(q_send, 2)
    kv_2 = shift(kv_x, quad)
    mates = [swap(after(a, kv_1), 1) for a in (kv_keep, kv_x)]
    mates += [swap(kv_1, 1), swap(kv_2, 1)]
    per = kv_keep.shape[1] // chunks

    sums, parts = [], []
    dq = ()
    for i in range(chunks):
        *dq, prev_here, prev_mate, own_here, own_mate = grads(
            i * per, per, tuple(dq), place, q_keep, q_x,
            kv_keep, kv_x, mates[0], mates[1], kv_1, kv_2, mates[2], mates[3],
        )
        sums.append((prev_here + swap(prev_mate, 1).astype(f32)).astype(bf))
        parts.append((own_here, own_mate))
    parts = [here + swap(after(mate, sums[0]), 1).astype(f32) for here, mate in parts]
    dq_x = swap(after(dq[1], sums[0]), 2)
    back_a = shift(sums[0], -quad)
    back_b2 = shift(sums[1][1], -quad)
    back_b1 = shift(sums[1][0], -quad)
    sum_a = parts[0] + back_a.astype(f32)
    send_a = sum_a[1].astype(bf)
    send_b = (parts[1][1] + after(back_b2, send_a).astype(f32)).astype(bf)
    other_a = swap(after(send_a, dq_x), 2)
    other_b = swap(after(send_b, send_a), 2)
    dq = join_heads(place, [[dq[0]]], [[after(dq_x, back_b1)]])
    dk, dv = join_heads(
        place, [[sum_a[0].astype(bf)], [parts[1][0], back_b1]], [[other_a], [other_b]]
    )
    return dq, dk, dv


def solution(mesh):
    spec = P("ctx", None, None)
    return jax.shard_map(
        body,
        mesh=mesh,
        in_specs=(spec,) * 4,
        out_specs=(spec,) * 3,
        check_vma=False,
    )
```
